32 devices in a mesh: group: 2 (over x), circ: 8 (over z, y), axial: 2 (over core).
Axes of the slice: x: 2, y: 2, z: 4, core: 2. Of those that a mesh axis runs over, the one named last changes fastest.
Arguments:
- features: bfloat16 [3, 8, 64, 128], P(None, ('group', 'axial'), 'circ'), parts along dimension 1, may hold values from -6 to 6
- w_first: bfloat16 [27, 64, 3], replicated, may hold values from -0.625 to 0.625
- w_middle: bfloat16 [27, 64, 64], replicated, may hold values from -0.15625 to 0.15625
- w_last: bfloat16 [27, 4, 64], replicated, may hold values from -0.15625 to 0.15625
- diffusion: float32 [3, 8, 64, 128], P(None, ('group', 'axial'), 'circ'), parts along dimension 1, may hold values from 0.3 to 3
- pressure: float32 [3, 8, 64, 128], P(None, ('group', 'axial'), 'circ'), parts along dimension 1, may hold values from 0.5 to 2
- advection: float32 [3, 8, 64, 128], P(None, ('group', 'axial'), 'circ'), parts along dimension 1, may hold values from -3 to 3
- forcing: float32 [3, 8, 64, 128], P(None, ('group', 'axial'), 'circ'), parts along dimension 1, may hold values from -6 to 6
Outputs:
- predicted: bfloat16 [4, 8, 64, 128], P(None, ('group', 'axial'), 'circ'), parts along dimension 1
- grad_first: float32 [54, 64, 3], P('group'), parts along dimension 0
- grad_middle: float32 [54, 64, 64], P('group'), parts along dimension 0
- grad_last: float32 [54, 4, 64], P('group'), parts along dimension 0
The draws below stay inside these ranges and needn't reach their ends.
There are 2 independent parts, one for each index of `group`. The reference program is written for one: setup_inputs(seed, part) draws one part's arguments, and reference() takes and returns one part's arrays. A program takes and returns all parts, laid end to end along the dimension named above; an argument that names none is the same for every part. Nothing has to cross between parts.
All inputs are finite; a program needn't handle non-finite values.
Results may differ from the reference program's by a relative error of at most 0.0056.
Values may be sent and summed in bfloat16 or wider, within the bound.
A program may use at most 64 MiB of HBM per device.

```python
import math
import jax
import jax.numpy as jnp

NR = 128
CH = 64
NIN = 3
NOUT = 4
NA = 4
NC = 64
NCELLS = 32768


def block_levels(own_key, dims, cuts, least, top_value):
    gain, own = 1.0, jax.random.fold_in(own_key, 6)
    for position, parts in cuts:
        draws = jnp.exp(jax.random.uniform(jax.random.fold_in(own, position), (parts,), jnp.float32, least / len(cuts), top_value / len(cuts)))
        gain = gain * jnp.repeat(draws, dims[position] // parts).reshape([-1 if axis == position else 1 for axis in range(len(dims))])
    return gain


def bell_draw(key, dims, deviation, bound, cuts=(), held_as=jnp.bfloat16):
    values = deviation * jax.random.normal(key, dims, jnp.float32)
    if cuts:
        values = values * block_levels(key, dims, cuts, -0.22, 0.18)
    return jnp.clip(values, -bound, bound).astype(held_as)


def setup_inputs(seed: int = 0, part: int = 0) -> dict:
    seeds = jax.random.split(jax.random.key(seed), 9)
    part_splits = jax.random.split(jax.random.fold_in(seeds[8], part), 9)
    features = bell_draw(part_splits[0], (NIN, NA, NC, NR), 1.0, 6.0, ((1, 2), (2, 8)))
    w_first = bell_draw(seeds[1], (27, CH, NIN), (27 * NIN) ** -0.5, 0.625)
    w_middle = bell_draw(seeds[2], (27, CH, CH), (27 * CH) ** -0.5, 0.15625)
    w_last = bell_draw(seeds[3], (27, NOUT, CH), (27 * CH) ** -0.5, 0.15625)
    diffusion = jnp.clip(jnp.exp(math.log(3.0) - 2.3025851 * jax.random.uniform(part_splits[4], (3, NA, NC, NR), jnp.float32) ** block_levels(part_splits[4], (3, NA, NC, NR), ((1, 2), (2, 8)), -0.2, 0.2)), 0.3, 3.0)
    pressure = jnp.clip(0.5 + 1.5 * jax.random.uniform(part_splits[5], (3, NA, NC, NR), jnp.float32) ** block_levels(part_splits[5], (3, NA, NC, NR), ((1, 2), (2, 8)), -0.2, 0.2), 0.5, 2.0)
    advection = bell_draw(part_splits[6], (3, NA, NC, NR), 0.5, 3.0, ((1, 2), (2, 8)), jnp.float32)
    forcing = bell_draw(part_splits[7], (3, NA, NC, NR), 1.0, 6.0, ((1, 2), (2, 8)), jnp.float32)
    return {"features": features, "w_first": w_first, "w_middle": w_middle, "w_last": w_last, "diffusion": diffusion, "pressure": pressure, "advection": advection, "forcing": forcing}


def extend(field):
    field = jnp.pad(field, ((0, 0), (1, 1), (0, 0), (1, 1)))
    return jnp.concatenate([field[:, :, -1:], field, field[:, :, :1]], axis=2)

def window(padded, offset, flipped):
    first_off = offset // 9
    second_off = offset // 3 % 3
    third_off = offset % 3
    if flipped:
        first_off, second_off, third_off = (2 - first_off, 2 - second_off, 2 - third_off)
    rows = padded.shape[1] - 2
    cols = padded.shape[2] - 2
    depth = padded.shape[3] - 2
    return padded[:, first_off:first_off + rows, second_off:second_off + cols, third_off:third_off + depth]

def convolve(padded, weights):
    total = None
    for offset in range(27):
        term = jnp.einsum('oi,iabr->oabr', weights[offset].astype(jnp.float32), window(padded, offset, False))
        total = term if total is None else total + term
    return total

def convolve_back(padded, weights):
    total = None
    for offset in range(27):
        term = jnp.einsum('oi,oabr->iabr', weights[offset].astype(jnp.float32), window(padded, offset, True))
        total = term if total is None else total + term
    return total

def weight_terms(cotangent, padded):
    terms = [jnp.einsum('oabr,iabr->oi', cotangent, window(padded, offset, False)) for offset in range(27)]
    return jnp.stack(terms)

def residual_core(padded, diffusion, pressure, advection, forcing):
    centre = padded[:, 1:-1, 1:-1, 1:-1]
    ahead = (padded[:, 2:, 1:-1, 1:-1], padded[:, 1:-1, 2:, 1:-1], padded[:, 1:-1, 1:-1, 2:])
    behind = (padded[:, :-2, 1:-1, 1:-1], padded[:, 1:-1, :-2, 1:-1], padded[:, 1:-1, 1:-1, :-2])
    velocity = centre[:3]
    result = forcing
    for direction in range(3):
        result = result + diffusion[direction] * (ahead[direction][:3] - 2.0 * velocity + behind[direction][:3])
        result = result - advection[direction] * velocity[direction] * (ahead[direction][:3] - behind[direction][:3]) * 0.5
    slopes = jnp.stack([ahead[direction][3] - behind[direction][3] for direction in range(3)]) * 0.5
    return result - pressure * slopes

def reference(features, w_first, w_middle, w_last, diffusion, pressure, advection, forcing):
    feat_pad = extend(features.astype(jnp.float32))
    first = jnp.tanh(convolve(feat_pad, w_first)).astype(jnp.bfloat16)
    first_pad = extend(first.astype(jnp.float32))
    middle = jnp.tanh(convolve(first_pad, w_middle)).astype(jnp.bfloat16)
    middle_pad = extend(middle.astype(jnp.float32))
    predicted = convolve(middle_pad, w_last).astype(jnp.bfloat16)

    def full_residual(field):
        return residual_core(extend(field), diffusion, pressure, advection, forcing)
    resid, pullback = jax.vjp(full_residual, predicted.astype(jnp.float32))
    out_grad, = pullback(resid / (3.0 * NCELLS))
    out_grad = out_grad.astype(jnp.bfloat16).astype(jnp.float32)
    grad_last = weight_terms(out_grad, middle_pad)
    middle_f = middle.astype(jnp.float32)
    middle_back = (convolve_back(extend(out_grad), w_last) * (1.0 - middle_f * middle_f)).astype(jnp.bfloat16).astype(jnp.float32)
    grad_middle = weight_terms(middle_back, first_pad)
    first_f = first.astype(jnp.float32)
    first_back = (convolve_back(extend(middle_back), w_middle) * (1.0 - first_f * first_f)).astype(jnp.bfloat16).astype(jnp.float32)
    grad_first = weight_terms(first_back, feat_pad)
    return (predicted, grad_first, grad_middle, grad_last)
```

```python
import functools

import jax
import jax.numpy as jnp
from jax import lax
from jax.experimental import pallas as pl
from jax.experimental.pallas import tpu as pltpu
from jax.sharding import PartitionSpec as P

MESH = pl.DeviceIdType.MESH
F32 = jnp.float32
BF16 = jnp.bfloat16
HALO = 4


def dot(a, b):
    return jnp.dot(a, b, preferred_element_type=F32)


def dot_nt(a, b):
    return lax.dot_general(a, b, (((1,), (1,)), ((), ())), preferred_element_type=F32)


def from_behind(x):
    axis = x.ndim - 1
    lane = lax.broadcasted_iota(jnp.int32, x.shape, axis) % 128
    return jnp.where(lane == 0, 0.0, pltpu.roll(x, 1, axis))


def from_ahead(x):
    axis = x.ndim - 1
    lane = lax.broadcasted_iota(jnp.int32, x.shape, axis) % 128
    return jnp.where(lane == 127, 0.0, pltpu.roll(x, x.shape[axis] - 1, axis))


def shift_sum(z, rows):
    return from_behind(z[0:rows]) + z[rows : 2 * rows] + from_ahead(z[2 * rows : 3 * rows])


def shift_sum_back(z, rows):
    return from_ahead(z[0:rows]) + z[rows : 2 * rows] + from_behind(z[2 * rows : 3 * rows])


def ahead(x, d):
    if d == 0:
        return jnp.concatenate([x[1:], jnp.zeros_like(x[:1])], axis=0)
    if d == 1:
        return pltpu.roll(x, 15, 1)
    return from_ahead(x)


def behind(x, d):
    if d == 0:
        return jnp.concatenate([jnp.zeros_like(x[:1]), x[:-1]], axis=0)
    if d == 1:
        return pltpu.roll(x, 1, 1)
    return from_behind(x)


def low_half(x, y):
    sub = lax.broadcasted_iota(jnp.int32, x.shape, x.ndim - 2)
    return jnp.where(sub < 4, x, y)


def roll4(x):
    return pltpu.roll(x, 4, x.ndim - 2)


def pack_low(x0, x1):
    return low_half(x0, roll4(x1))


def pack_high(x0, x1):
    return low_half(roll4(x1), x0)


def halo_tiles(right, left):
    return low_half(right, left), roll4(low_half(left, right))


def kernel(n, cells, chunk, fchunk, *refs):
    (feat, wf, wb, w1, w3, w3t, diff, pres, adv, forc,
     pred_out, gfirst_out, gmid_out, glast_out,
     fc, fr, fl, mc, mr, ml, fsend, msend, fbase, fstage, fs, f1x, mid, m1x, pc, ph, psend,
     ogs, obase, og, mbx, fbs,
     red, redin, half, hin, gat, gfp, gfin, gfr,
     a_send, a_recv, p_send, p_recv, r_send, r_recv, s_send, s_recv, g_send, g_recv,
     x_send, x_recv, q_send, q_recv, h_send, h_recv) = refs
    c = lax.axis_index("circ")
    ax = lax.axis_index("axial")
    grp = lax.axis_index("group")
    sib = 1 - ax
    right = lax.rem(c + 1, n)
    left = lax.rem(c + n - 1, n)
    ndev = 2 * n
    me = c * 2 + ax

    def device(i):
        return (grp, i // 2, lax.rem(i, 2))

    def rcopy(src, dst, ss, rs, circ, axial):
        return pltpu.make_async_remote_copy(
            src_ref=src, dst_ref=dst, send_sem=ss, recv_sem=rs,
            device_id=(grp, circ, axial), device_id_type=MESH)

    barrier = pltpu.get_barrier_semaphore()

    def greet(j, carry):
        pl.semaphore_signal(barrier, inc=1, device_id=device(lax.rem(me + j, ndev)), device_id_type=MESH)
        return carry

    lax.fori_loop(1, ndev, greet, 0)

    x = feat[...].astype(F32)
    fc[ax] = x
    fsend[0] = pack_low(x[:, 0], x[:, 1])
    fsend[1] = pack_high(x[:, 0], x[:, 1])
    for g, ref in enumerate((diff, pres, adv, forc)):
        x = ref[...]
        mc[ax, 3 * g : 3 * g + 3] = x
        msend[0, 3 * g : 3 * g + 3] = pack_low(x[:, 0], x[:, 1])
        msend[1, 3 * g : 3 * g + 3] = pack_high(x[:, 0], x[:, 1])

    pl.semaphore_wait(barrier, ndev - 1)

    fcopies = []
    mcopies = []
    for out, cc, src_f, src_m, base in (
        (fcopies, fc, None, None, 0), (mcopies, mc, None, None, 5)):
        out.append(rcopy(cc.at[ax], cc.at[ax], a_send.at[base], a_recv.at[base], c, sib))
    for out, lo, hi, snd, base in ((fcopies, fr, fl, fsend, 0), (mcopies, mr, ml, msend, 5)):
        out.append(rcopy(snd.at[0], lo.at[ax], a_send.at[base + 1], a_recv.at[base + 1], left, ax))
        out.append(rcopy(snd.at[1], hi.at[ax], a_send.at[base + 2], a_recv.at[base + 2], right, ax))
        out.append(rcopy(snd.at[0], lo.at[ax], a_send.at[base + 3], a_recv.at[base + 3], left, sib))
        out.append(rcopy(snd.at[1], hi.at[ax], a_send.at[base + 4], a_recv.at[base + 4], right, sib))
    for cp in fcopies + mcopies:
        cp.start()

    for ref in (fs, f1x, m1x, og, mbx):
        ref[0] = jnp.zeros_like(ref[0])
        ref[5] = jnp.zeros_like(ref[5])
    fstage[...] = jnp.zeros_like(fstage)
    red[944:1024] = jnp.zeros((80, 128), BF16)
    gfp[...] = jnp.zeros_like(gfp)
    fbase[...] = jnp.zeros_like(fbase)
    obase[...] = jnp.zeros_like(obase)

    for cp in fcopies:
        cp.wait()

    for a in range(4):
        slab, l = a // 2, a % 2
        for ch in range(3):
            for j in range(14):
                b = j - 3
                if b < 0:
                    row = (8 + b) - 4 + (4 if l == 0 else 0)
                    v = fl[slab, ch, row : row + 1, :]
                elif b > 7:
                    row = (b - 8) + 4 * l
                    v = fr[slab, ch, row : row + 1, :]
                else:
                    v = fc[slab, ch, l, b : b + 1, :]
                fbase[a, ch : ch + 1, j * 128 : (j + 1) * 128] = v
        base = fbase[a]
        fstage[0:3, :] = from_behind(base)[0:3]
        fstage[3:6, :] = base[0:3]
        fstage[6:9, :] = from_ahead(base)[0:3]
        fs[a + 1] = fstage[...].astype(BF16)

    for a in range(4):
        xs = jnp.concatenate(
            [fs[a + da, :, db * 128 : db * 128 + 1536] for da in range(3) for db in range(3)], axis=0)
        first = jnp.tanh(dot(w1[...], xs)).astype(BF16)
        for db in range(3):
            f1x[a + 1, db * 64 : db * 64 + 64, :] = first[:, db * 128 : db * 128 + 1280]

    for a in range(4):
        for t in range(5):
            acc = None
            for da in range(3):
                if 0 <= a + da - 1 < 4:
                    term = dot(wf[da], f1x[a + da, :, t * 256 : t * 256 + 256])
                    acc = term if acc is None else acc + term
            mid[a, :, t * 256 : t * 256 + 256] = jnp.tanh(shift_sum(acc, 64)).astype(BF16)
        for db in range(3):
            m1x[a + 1, db * 64 : db * 64 + 64, :] = mid[a, :, db * 128 : db * 128 + 1024]

    for a in range(4):
        acc = None
        for da in range(3):
            if 0 <= a + da - 1 < 4:
                term = dot(w3[da], m1x[a + da])
                acc = term if acc is None else acc + term
        y = shift_sum(acc, 8).astype(BF16).astype(F32)
        for ch in range(4):
            for b in range(8):
                pc[ch, a, b : b + 1, :] = y[ch : ch + 1, b * 128 : b * 128 + 128]
    q = pc[...]
    for s in range(2):
        psend[0, :, s] = pack_low(q[:, 2 * s], q[:, 2 * s + 1])
        psend[1, :, s] = pack_high(q[:, 2 * s], q[:, 2 * s + 1])
    pcopies = [
        rcopy(psend.at[0], ph.at[0], p_send.at[0], p_recv.at[0], left, ax),
        rcopy(psend.at[1], ph.at[1], p_send.at[1], p_recv.at[1], right, ax),
    ]
    for cp in pcopies:
        cp.start()
    pred_out[...] = pc[:, pl.ds(2 * ax, 2)].astype(BF16)
    for cp in mcopies:
        cp.wait()
    for cp in pcopies:
        cp.wait()

    def metric(index):
        layers = []
        for slab in range(2):
            h = halo_tiles(mr[slab, index], ml[slab, index])
            for l in range(2):
                layers.append(jnp.concatenate([mc[slab, index, l], h[l]], axis=0))
        return jnp.stack(layers)

    field = []
    for ch in range(4):
        layers = []
        for s in range(2):
            h = halo_tiles(ph[0, ch, s], ph[1, ch, s])
            for l in range(2):
                layers.append(jnp.concatenate([pc[ch, 2 * s + l], h[l]], axis=0))
        field.append(jnp.stack(layers))
    D = [metric(d) for d in range(3)]
    A = [metric(6 + d) for d in range(3)]
    resid = [metric(9 + m) for m in range(3)]
    pm = [metric(3 + m) for m in range(3)]
    diffs = {}
    for m in range(3):
        for d in range(3):
            pa, pb = ahead(field[m], d), behind(field[m], d)
            diffs[m, d] = (pa - pb) * 0.5
            resid[m] = resid[m] + D[d] * (pa - 2.0 * field[m] + pb) - A[d] * field[d] * diffs[m, d]
        resid[m] = resid[m] - pm[m] * (ahead(field[3], m) - behind(field[3], m)) * 0.5
    t = [r / (3.0 * cells) for r in resid]
    out_p = None
    for m in range(3):
        total = None
        for d in range(3):
            dt = D[d] * t[m]
            y = A[d] * field[d] * t[m] * 0.5
            term = ahead(dt + y, d) + behind(dt - y, d) - 2.0 * dt
            total = term if total is None else total + term
        total = total - A[m] * (t[0] * diffs[0, m] + t[1] * diffs[1, m] + t[2] * diffs[2, m])
        ogs[m] = total
        y = pm[m] * t[m] * 0.5
        term = ahead(y, m) - behind(y, m)
        out_p = term if out_p is None else out_p + term
    ogs[3] = out_p

    fstage[0:16, :] = jnp.zeros((16, 1792), F32)
    for a in range(4):
        for ch in range(4):
            for j in range(12):
                b = (j - 2) % 16
                obase[a, ch : ch + 1, j * 128 : (j + 1) * 128] = ogs[ch, a, b : b + 1, :]
        base = obase[a]
        fstage[0:4, 0:1536] = from_ahead(base)[0:4]
        fstage[4:8, 0:1536] = base[0:4]
        fstage[8:12, 0:1536] = from_behind(base)[0:4]
        og[a + 1] = fstage[:, 0:1536].astype(BF16)

    for a in range(4):
        xs = jnp.concatenate(
            [og[a + 2 - da, :, (2 - db) * 128 : (2 - db) * 128 + 1280] for da in range(3) for db in range(3)],
            axis=0)
        mf = mid[a].astype(F32)
        back = (dot(w3t[...], xs) * (1.0 - mf * mf)).astype(BF16)
        for db in range(3):
            mbx[a + 1, db * 64 : db * 64 + 64, :] = back[:, (2 - db) * 128 : (2 - db) * 128 + 1024]

    own = 2 * ax + 1
    gm = [None] * 3
    gl = [None] * 3
    for l in range(2):
        m = mbx[own + l, 64:128, :].astype(F32)
        mbs = jnp.concatenate([from_ahead(m), m, from_behind(m)], axis=0).astype(BF16)
        ogo = og[own + l, :, 256:1280]
        for da in range(3):
            term = dot_nt(mbs, f1x[own + l + da - 1, :, 128:1152])
            gm[da] = term if gm[da] is None else gm[da] + term
            term = dot_nt(ogo, m1x[own + l + da - 1])
            gl[da] = term if gl[da] is None else gl[da] + term

    def block(parts, dd):
        return parts[dd // 3][:, dd % 3 * 64 : dd % 3 * 64 + 64]

    for p in range(4):
        red[p * 192 : p * 192 + 192] = jnp.concatenate(
            [block(gm, 2 * p), block(gm, 2 * p + 1)], axis=1).astype(BF16)
        red[864 + p * 16 : 880 + p * 16] = jnp.concatenate(
            [block(gl, 2 * p), block(gl, 2 * p + 1)], axis=1).astype(BF16)
    lastm, lastl = block(gm, 8), block(gl, 8)
    red[768:864] = jnp.concatenate([lastm[0:96], lastm[96:192]], axis=1).astype(BF16)
    red[928:944] = jnp.concatenate([lastl, jnp.zeros_like(lastl)], axis=1).astype(BF16)

    hrows = red.shape[0] // 2
    swap = rcopy(red.at[pl.ds(pl.multiple_of(sib * hrows, 16), hrows)], redin, r_send, r_recv, c, sib)
    swap.start()

    def first_back(l):
        acc = None
        for da in range(3):
            term = dot(wb[da], mbx[own + l + 1 - da])
            acc = term if acc is None else acc + term
        ff = f1x[own + l, 64:128, 128:1152].astype(F32)
        return (shift_sum_back(acc, 64) * (1.0 - ff * ff)).astype(BF16)

    fbs[0] = first_back(0)
    swap.wait()
    half[...] = (red[pl.ds(pl.multiple_of(ax * hrows, 16), hrows)].astype(F32) + redin[...].astype(F32)).astype(BF16)

    def scatter(j):
        peer = lax.rem(c + j, n)
        return rcopy(half.at[pl.ds(pl.multiple_of(peer * chunk, 16), chunk)], hin.at[j],
                     s_send.at[j], s_recv.at[j], peer, ax)

    def start_scatter(j, carry):
        scatter(j).start()
        return carry

    lax.fori_loop(1, n, start_scatter, 0)

    fbs[1] = first_back(1)
    gf = None
    for l in range(2):
        xs = jnp.concatenate(
            [fs[own + l + da - 1, :, (2 + db) * 128 : (2 + db) * 128 + 1024]
             for da in range(3) for db in range(3)], axis=0)
        term = dot_nt(fbs[l], xs)
        gf = term if gf is None else gf + term
    gfp[0:64, :] = gf[:, 0:128]
    gfp[64:128, 0:16] = gf[:, 128:144]

    def fscatter(j):
        peer = lax.rem(me + j, ndev)
        return pltpu.make_async_remote_copy(
            src_ref=gfp.at[pl.ds(pl.multiple_of(peer * fchunk, 8), fchunk)], dst_ref=gfin.at[j],
            send_sem=x_send.at[j], recv_sem=x_recv.at[j], device_id=device(peer), device_id_type=MESH)

    def start_fscatter(j, carry):
        fscatter(j).start()
        return carry

    lax.fori_loop(1, ndev, start_fscatter, 0)

    def add_chunk(j, total):
        scatter(j).wait()
        return total + hin[j].astype(F32)

    mine = half[pl.ds(pl.multiple_of(c * chunk, 16), chunk)].astype(F32)
    total = lax.fori_loop(1, n, add_chunk, mine)
    here = pl.multiple_of(c * chunk, 16)
    gat[ax, pl.ds(here, chunk)] = total.astype(BF16)

    def gather(j):
        part = gat.at[ax, pl.ds(here, chunk)]
        return rcopy(part, part, g_send.at[j], g_recv.at[j], lax.rem(c + j, n), ax)

    def start_gather(j, carry):
        gather(j).start()
        return carry

    lax.fori_loop(1, n, start_gather, 0)

    def forward(j):
        origin = lax.rem(c + n - j, n)
        part = gat.at[ax, pl.ds(pl.multiple_of(origin * chunk, 16), chunk)]
        return rcopy(part, part, h_send.at[j], h_recv.at[j], c, sib)

    forward(0).start()

    def fadd(j, total):
        fscatter(j).wait()
        return total + gfin[j]

    fmine = gfp[pl.ds(pl.multiple_of(me * fchunk, 8), fchunk)]
    fhere = pl.multiple_of(me * fchunk, 8)
    gfr[pl.ds(fhere, fchunk)] = lax.fori_loop(1, ndev, fadd, fmine)

    def fgather(j):
        peer = lax.rem(me + j, ndev)
        part = gfr.at[pl.ds(fhere, fchunk)]
        return pltpu.make_async_remote_copy(
            src_ref=part, dst_ref=part, send_sem=q_send.at[j], recv_sem=q_recv.at[j],
            device_id=device(peer), device_id_type=MESH)

    def start_fgather(j, carry):
        fgather(j).start()
        return carry

    lax.fori_loop(1, ndev, start_fgather, 0)

    def relay(j, carry):
        gather(j).wait()
        forward(j).start()
        return carry

    lax.fori_loop(1, n, relay, 0)

    def end_forward(j, carry):
        forward(j).wait()
        return carry

    lax.fori_loop(0, n, end_forward, 0)

    def rows_of(start, count, lanes):
        hr = hrows
        if start + count <= hr:
            return gat[0, start : start + count, lanes : lanes + 64]
        if start >= hr:
            return gat[1, start - hr : start - hr + count, lanes : lanes + 64]
        return jnp.concatenate(
            [gat[0, start:hr, lanes : lanes + 64], gat[1, 0 : start + count - hr, lanes : lanes + 64]], axis=0)

    for dd in range(9):
        if dd < 8:
            lblock = rows_of(864 + dd // 2 * 16, 16, dd % 2 * 64).astype(F32)
        else:
            lblock = rows_of(928, 16, 0).astype(F32)
        for dr in range(3):
            k = dd * 3 + dr
            glast_out[k] = lblock[dr * 4 : dr * 4 + 4]
            if dd < 8:
                gmid_out[k] = rows_of(dd // 2 * 192 + dr * 64, 64, dd % 2 * 64).astype(F32)
            elif dr == 0:
                gmid_out[k] = rows_of(768, 64, 0).astype(F32)
            elif dr == 1:
                gmid_out[k, 0:32] = rows_of(832, 32, 0).astype(F32)
                gmid_out[k, 32:64] = rows_of(768, 32, 64).astype(F32)
            else:
                gmid_out[k] = rows_of(800, 64, 64).astype(F32)

    def end_fgather(j, carry):
        fgather(j).wait()
        return carry

    lax.fori_loop(1, ndev, end_fgather, 0)
    g0 = gfr[0:64, :]
    g1 = gfr[64:128, :]
    for dd in range(9):
        src = g0 if dd < 8 else g1
        for dr in range(3):
            start = (dd * 16) % 128 + dr * 3
            gfirst_out[dd * 3 + dr] = src[:, start : start + 3]


def body(features, w_first, w_middle, w_last, diffusion, pressure, advection, forcing):
    n = lax.axis_size("circ")
    ndev = 2 * n
    rows, cols, depth = features.shape[1:]
    cells = rows * cols * depth * ndev
    chunk = max(16, 512 // n)
    rrows = chunk * n * 2
    fchunk = max(8, 128 // ndev)
    frows = fchunk * ndev

    w = w_middle.reshape(3, 3, 3, 64, 64)
    wf = w.transpose(0, 2, 3, 1, 4).reshape(3, 192, 192)
    wb = w.transpose(0, 2, 4, 1, 3).reshape(3, 192, 192)
    w1 = w_first.reshape(3, 3, 3, 64, 3).transpose(3, 0, 1, 2, 4).reshape(64, 9, 9)
    w1 = jnp.pad(w1, ((0, 0), (0, 0), (0, 7))).reshape(64, 144)
    wl = w_last.reshape(3, 3, 3, 4, 64)
    w3 = jnp.pad(wl.transpose(0, 2, 3, 1, 4), ((0, 0), (0, 0), (0, 4), (0, 0), (0, 0))).reshape(3, 24, 192)
    w3 = jnp.pad(w3, ((0, 0), (0, 8), (0, 0)))
    w3t = wl.transpose(4, 0, 1, 2, 3).reshape(64, 9, 12)
    w3t = jnp.pad(w3t, ((0, 0), (0, 0), (0, 4))).reshape(64, 144)

    V = pltpu.VMEM
    dma = pltpu.SemaphoreType.DMA
    scratch = [
        V((2, 3, 2, 8, 128), F32), V((2, 3, 8, 128), F32), V((2, 3, 8, 128), F32),
        V((2, 12, 2, 8, 128), F32), V((2, 12, 8, 128), F32), V((2, 12, 8, 128), F32),
        V((2, 3, 8, 128), F32), V((2, 12, 8, 128), F32),
        V((4, 8, 1792), F32), V((16, 1792), F32), V((6, 16, 1792), BF16),
        V((6, 192, 1280), BF16), V((4, 64, 1280), BF16), V((6, 192, 1024), BF16),
        V((4, 4, 8, 128), F32), V((2, 4, 2, 8, 128), F32), V((2, 4, 2, 8, 128), F32),
        V((4, 4, 16, 128), F32), V((4, 8, 1536), F32), V((6, 16, 1536), BF16),
        V((6, 192, 1024), BF16), V((2, 64, 1024), BF16),
        V((rrows, 128), BF16), V((rrows // 2, 128), BF16), V((rrows // 2, 128), BF16),
        V((n, chunk, 128), BF16), V((2, rrows // 2, 128), BF16),
        V((frows, 128), F32), V((ndev, fchunk, 128), F32), V((frows, 128), F32),
        dma((10,)), dma((10,)), dma((2,)), dma((2,)), dma, dma, dma((n,)), dma((n,)), dma((n,)), dma((n,)),
        dma((ndev,)), dma((ndev,)), dma((ndev,)), dma((ndev,)), dma((n,)), dma((n,)),
    ]
    vm = pl.BlockSpec(memory_space=pltpu.VMEM)
    return pl.pallas_call(
        functools.partial(kernel, n, cells, chunk, fchunk),
        out_shape=(
            jax.ShapeDtypeStruct((4, rows, cols, depth), BF16),
            jax.ShapeDtypeStruct((27, 64, 3), F32),
            jax.ShapeDtypeStruct((27, 64, 64), F32),
            jax.ShapeDtypeStruct((27, 4, 64), F32),
        ),
        in_specs=[vm] * 10,
        out_specs=(vm,) * 4,
        scratch_shapes=scratch,
        compiler_params=pltpu.CompilerParams(
            collective_id=0, has_side_effects=True, vmem_limit_bytes=48 * 1024 * 1024),
    )(features, wf, wb, w1, w3, w3t, diffusion, pressure, advection, forcing)


def solution(mesh):
    field = P(None, ("group", "axial"), "circ", None)
    grad = P("group", None, None)
    return jax.shard_map(
        body,
        mesh=mesh,
        in_specs=(field, P(), P(), P(), field, field, field, field),
        out_specs=(field, grad, grad, grad),
        check_vma=False,
    )
```

```python
import functools

import jax
import jax.numpy as jnp
from jax import lax
from jax.experimental import pallas as pl
from jax.experimental.pallas import tpu as pltpu
from jax.sharding import PartitionSpec as P

MESH = pl.DeviceIdType.MESH
F32 = jnp.float32
BF16 = jnp.bfloat16
HALO = 4


def dot(a, b):
    return jnp.dot(a, b, preferred_element_type=F32)


def dot_nt(a, b):
    return lax.dot_general(a, b, (((1,), (1,)), ((), ())), preferred_element_type=F32)


def from_behind(x):
    axis = x.ndim - 1
    lane = lax.broadcasted_iota(jnp.int32, x.shape, axis) % 128
    return jnp.where(lane == 0, 0.0, pltpu.roll(x, 1, axis))


def from_ahead(x):
    axis = x.ndim - 1
    lane = lax.broadcasted_iota(jnp.int32, x.shape, axis) % 128
    return jnp.where(lane == 127, 0.0, pltpu.roll(x, x.shape[axis] - 1, axis))


def shift_sum(z, rows):
    return from_behind(z[0:rows]) + z[rows : 2 * rows] + from_ahead(z[2 * rows : 3 * rows])


def shift_sum_back(z, rows):
    return from_ahead(z[0:rows]) + z[rows : 2 * rows] + from_behind(z[2 * rows : 3 * rows])


def ahead(x, d):
    if d == 0:
        return jnp.concatenate([x[1:], jnp.zeros_like(x[:1])], axis=0)
    if d == 1:
        return pltpu.roll(x, 15, 1)
    return from_ahead(x)


def behind(x, d):
    if d == 0:
        return jnp.concatenate([jnp.zeros_like(x[:1]), x[:-1]], axis=0)
    if d == 1:
        return pltpu.roll(x, 1, 1)
    return from_behind(x)


def low_half(x, y):
    sub = lax.broadcasted_iota(jnp.int32, x.shape, x.ndim - 2)
    return jnp.where(sub < 4, x, y)


def roll4(x):
    return pltpu.roll(x, 4, x.ndim - 2)


def pack_low(x0, x1):
    return low_half(x0, roll4(x1))


def pack_high(x0, x1):
    return low_half(roll4(x1), x0)


def halo_tiles(right, left):
    return low_half(right, left), roll4(low_half(left, right))


def kernel(n, cells, chunk, fchunk, *refs):
    (feat, w1_in, wm_in, wl_in, diff, pres, adv, forc,
     pred_out, gf_out, gat_out,
     wf, wb, w1, w3, w3t, stage, w3s,
     fc, fr, fl, mc, mr, ml, fsend, msend, fbase, fstage, fs, f1x, mid, m1x, pc, ph, psend,
     ogs, obase, og, mbx, fbs,
     red, redin, half, hin, gat, gfp, gfin, gfr,
     a_send, a_recv, p_send, p_recv, r_send, r_recv, s_send, s_recv, g_send, g_recv,
     x_send, x_recv, q_send, q_recv, h_send, h_recv, m_send, m_recv) = refs
    c = lax.axis_index("circ")
    ax = lax.axis_index("axial")
    grp = lax.axis_index("group")
    sib = 1 - ax
    right = lax.rem(c + 1, n)
    left = lax.rem(c + n - 1, n)
    ndev = 2 * n
    me = c * 2 + ax

    def device(i):
        return (grp, i // 2, lax.rem(i, 2))

    def rcopy(src, dst, ss, rs, circ, axial):
        return pltpu.make_async_remote_copy(
            src_ref=src, dst_ref=dst, send_sem=ss, recv_sem=rs,
            device_id=(grp, circ, axial), device_id_type=MESH)

    barrier = pltpu.get_barrier_semaphore()

    def greet(j, carry):
        pl.semaphore_signal(barrier, inc=1, device_id=device(lax.rem(me + j, ndev)), device_id_type=MESH)
        return carry

    lax.fori_loop(1, ndev, greet, 0)

    x = feat[...].astype(F32)
    fc[ax] = x
    fsend[0] = pack_low(x[:, 0], x[:, 1])
    fsend[1] = pack_high(x[:, 0], x[:, 1])
    lows, highs = [], []
    for g, ref in enumerate((diff, pres, adv, forc)):
        x = ref[...]
        mc[ax, 3 * g : 3 * g + 3] = x
        for i in range(3):
            lows.append(pack_low(x[i, 0], x[i, 1]))
            highs.append(pack_high(x[i, 0], x[i, 1]))
    for i in range(6):
        msend[0, i] = jnp.concatenate(lows[2 * i : 2 * i + 2], axis=0).astype(BF16)
        msend[1, i] = jnp.concatenate(highs[2 * i : 2 * i + 2], axis=0).astype(BF16)

    stage[...] = jnp.zeros_like(stage)
    for ch in range(3):
        v = w1_in[ch].astype(F32)
        for dd in range(9):
            stage[dd * 16 + ch * 3 : dd * 16 + ch * 3 + 3, 0:64] = v[3 * dd : 3 * dd + 3]
    w1[...] = stage[...].T[0:64].astype(BF16)

    pl.semaphore_wait(barrier, ndev - 1)

    fcopies = []
    mcopies = []
    fcopies.append(rcopy(fc.at[ax], fc.at[ax], a_send.at[0], a_recv.at[0], c, sib))
    fcopies.append(rcopy(fsend.at[0], fr.at[ax], a_send.at[1], a_recv.at[1], left, ax))
    fcopies.append(rcopy(fsend.at[1], fl.at[ax], a_send.at[2], a_recv.at[2], right, ax))
    fcopies.append(rcopy(fsend.at[0], fr.at[ax], a_send.at[3], a_recv.at[3], left, sib))
    fcopies.append(rcopy(fsend.at[1], fl.at[ax], a_send.at[4], a_recv.at[4], right, sib))
    mcopies.append(rcopy(mc.at[ax], mc.at[ax], a_send.at[5], a_recv.at[5], c, sib))
    mcopies.append(rcopy(msend.at[0], mr.at[ax], a_send.at[6], a_recv.at[6], left, ax))
    mcopies.append(rcopy(msend.at[1], ml.at[ax], a_send.at[7], a_recv.at[7], right, ax))
    relays = [
        rcopy(mr.at[ax], mr.at[ax], m_send.at[0], m_recv.at[0], c, sib),
        rcopy(ml.at[ax], ml.at[ax], m_send.at[1], m_recv.at[1], c, sib),
    ]
    for cp in fcopies + mcopies:
        cp.start()

    for da in range(3):
        for dr in range(3):
            wf[da, dr * 64 : dr * 64 + 64] = jnp.concatenate(
                [wm_in[9 * da + 3 * db + dr] for db in range(3)], axis=1)
    w3s[...] = jnp.zeros_like(w3s)
    for da in range(3):
        for dr in range(3):
            w3s[da, dr * 8 : dr * 8 + 4] = jnp.concatenate(
                [wl_in[9 * da + 3 * db + dr].astype(F32) for db in range(3)], axis=1)
    w3[...] = w3s[...].astype(BF16)

    for ref in (fs, f1x, m1x, og, mbx):
        ref[0] = jnp.zeros_like(ref[0])
        ref[5] = jnp.zeros_like(ref[5])
    fstage[...] = jnp.zeros_like(fstage)
    red[944:1024] = jnp.zeros((80, 128), BF16)
    gfp[...] = jnp.zeros_like(gfp)
    fbase[...] = jnp.zeros_like(fbase)
    obase[...] = jnp.zeros_like(obase)

    for cp in fcopies:
        cp.wait()

    for a in range(4):
        slab, l = a // 2, a % 2
        for ch in range(3):
            for j in range(14):
                b = j - 3
                if b < 0:
                    row = (8 + b) - 4 + (4 if l == 0 else 0)
                    v = fl[slab, ch, row : row + 1, :]
                elif b > 7:
                    row = (b - 8) + 4 * l
                    v = fr[slab, ch, row : row + 1, :]
                else:
                    v = fc[slab, ch, l, b : b + 1, :]
                fbase[a, ch : ch + 1, j * 128 : (j + 1) * 128] = v
        base = fbase[a]
        low, high = from_behind(base), from_ahead(base)
        for ch in range(3):
            fstage[3 * ch : 3 * ch + 1, :] = low[ch : ch + 1]
            fstage[3 * ch + 1 : 3 * ch + 2, :] = base[ch : ch + 1]
            fstage[3 * ch + 2 : 3 * ch + 3, :] = high[ch : ch + 1]
        fs[a + 1] = fstage[...].astype(BF16)

    for a in range(4):
        xs = jnp.concatenate(
            [fs[a + da, :, db * 128 : db * 128 + 1536] for da in range(3) for db in range(3)], axis=0)
        first = jnp.tanh(dot(w1[...], xs)).astype(BF16)
        for db in range(3):
            f1x[a + 1, db * 64 : db * 64 + 64, :] = first[:, db * 128 : db * 128 + 1280]

    for cp in mcopies:
        cp.wait()
    for cp in relays:
        cp.start()

    for a in range(4):
        for t in range(5):
            acc = None
            for da in range(3):
                if 0 <= a + da - 1 < 4:
                    term = dot(wf[da], f1x[a + da, :, t * 256 : t * 256 + 256])
                    acc = term if acc is None else acc + term
            mid[a, :, t * 256 : t * 256 + 256] = jnp.tanh(shift_sum(acc, 64)).astype(BF16)
        for db in range(3):
            m1x[a + 1, db * 64 : db * 64 + 64, :] = mid[a, :, db * 128 : db * 128 + 1024]

    for a in range(4):
        acc = None
        for da in range(3):
            if 0 <= a + da - 1 < 4:
                term = dot(w3[da], m1x[a + da])
                acc = term if acc is None else acc + term
        y = shift_sum(acc, 8).astype(BF16).astype(F32)
        for ch in range(4):
            for b in range(8):
                pc[ch, a, b : b + 1, :] = y[ch : ch + 1, b * 128 : b * 128 + 128]
    q = pc[...]
    for s in range(2):
        psend[0, :, s] = pack_low(q[:, 2 * s], q[:, 2 * s + 1])
        psend[1, :, s] = pack_high(q[:, 2 * s], q[:, 2 * s + 1])
    pcopies = [
        rcopy(psend.at[0], ph.at[0], p_send.at[0], p_recv.at[0], left, ax),
        rcopy(psend.at[1], ph.at[1], p_send.at[1], p_recv.at[1], right, ax),
    ]
    for cp in pcopies:
        cp.start()
    pred_out[...] = pc[:, pl.ds(2 * ax, 2)].astype(BF16)
    for dd in range(9):
        for dr in range(3):
            stage[dd * 16 + dr * 4 : dd * 16 + dr * 4 + 4, 0:64] = wl_in[dd * 3 + dr].astype(F32)
        stage[dd * 16 + 12 : dd * 16 + 16, 0:64] = jnp.zeros((4, 64), F32)
    w3t[...] = stage[...].T[0:64].astype(BF16)
    for da in range(3):
        for dr in range(3):
            tall = jnp.concatenate([wm_in[9 * da + 3 * db + dr] for db in range(3)], axis=0)
            wb[da, dr * 64 : dr * 64 + 64] = tall.T
    for cp in relays:
        cp.wait()
    for cp in pcopies:
        cp.wait()

    def metric(index):
        layers = []
        for slab in range(2):
            h = halo_tiles(*(ref[slab, index // 2].astype(F32)[index % 2 * 8 : index % 2 * 8 + 8] for ref in (mr, ml)))
            for l in range(2):
                layers.append(jnp.concatenate([mc[slab, index, l], h[l]], axis=0))
        return jnp.stack(layers)

    field = []
    for ch in range(4):
        layers = []
        for s in range(2):
            h = halo_tiles(ph[0, ch, s], ph[1, ch, s])
            for l in range(2):
                layers.append(jnp.concatenate([pc[ch, 2 * s + l], h[l]], axis=0))
        field.append(jnp.stack(layers))
    D = [metric(d) for d in range(3)]
    A = [metric(6 + d) for d in range(3)]
    resid = [metric(9 + m) for m in range(3)]
    pm = [metric(3 + m) for m in range(3)]
    diffs = {}
    for m in range(3):
        for d in range(3):
            pa, pb = ahead(field[m], d), behind(field[m], d)
            diffs[m, d] = (pa - pb) * 0.5
            resid[m] = resid[m] + D[d] * (pa - 2.0 * field[m] + pb) - A[d] * field[d] * diffs[m, d]
        resid[m] = resid[m] - pm[m] * (ahead(field[3], m) - behind(field[3], m)) * 0.5
    t = [r / (3.0 * cells) for r in resid]
    out_p = None
    for m in range(3):
        total = None
        for d in range(3):
            dt = D[d] * t[m]
            y = A[d] * field[d] * t[m] * 0.5
            term = ahead(dt + y, d) + behind(dt - y, d) - 2.0 * dt
            total = term if total is None else total + term
        total = total - A[m] * (t[0] * diffs[0, m] + t[1] * diffs[1, m] + t[2] * diffs[2, m])
        ogs[m] = total
        y = pm[m] * t[m] * 0.5
        term = ahead(y, m) - behind(y, m)
        out_p = term if out_p is None else out_p + term
    ogs[3] = out_p

    fstage[0:16, :] = jnp.zeros((16, 1792), F32)
    for a in range(4):
        for ch in range(4):
            for j in range(12):
                b = (j - 2) % 16
                obase[a, ch : ch + 1, j * 128 : (j + 1) * 128] = ogs[ch, a, b : b + 1, :]
        base = obase[a]
        fstage[0:4, 0:1536] = from_ahead(base)[0:4]
        fstage[4:8, 0:1536] = base[0:4]
        fstage[8:12, 0:1536] = from_behind(base)[0:4]
        og[a + 1] = fstage[:, 0:1536].astype(BF16)

    for a in range(4):
        xs = jnp.concatenate(
            [og[a + 2 - da, :, (2 - db) * 128 : (2 - db) * 128 + 1280] for da in range(3) for db in range(3)],
            axis=0)
        mf = mid[a].astype(F32)
        back = (dot(w3t[...], xs) * (1.0 - mf * mf)).astype(BF16)
        for db in range(3):
            mbx[a + 1, db * 64 : db * 64 + 64, :] = back[:, (2 - db) * 128 : (2 - db) * 128 + 1024]

    own = 2 * ax + 1
    gm = [None] * 3
    gl = [None] * 3
    for l in range(2):
        m = mbx[own + l, 64:128, :].astype(F32)
        mbs = jnp.concatenate([from_ahead(m), m, from_behind(m)], axis=0).astype(BF16)
        ogo = og[own + l, :, 256:1280]
        for da in range(3):
            term = dot_nt(mbs, f1x[own + l + da - 1, :, 128:1152])
            gm[da] = term if gm[da] is None else gm[da] + term
            term = dot_nt(ogo, m1x[own + l + da - 1])
            gl[da] = term if gl[da] is None else gl[da] + term

    def block(parts, dd):
        return parts[dd // 3][:, dd % 3 * 64 : dd % 3 * 64 + 64]

    for p in range(4):
        red[p * 192 : p * 192 + 192] = jnp.concatenate(
            [block(gm, 2 * p), block(gm, 2 * p + 1)], axis=1).astype(BF16)
        red[864 + p * 16 : 880 + p * 16] = jnp.concatenate(
            [block(gl, 2 * p), block(gl, 2 * p + 1)], axis=1).astype(BF16)
    lastm, lastl = block(gm, 8), block(gl, 8)
    red[768:864] = jnp.concatenate([lastm[0:96], lastm[96:192]], axis=1).astype(BF16)
    red[928:944] = jnp.concatenate([lastl, jnp.zeros_like(lastl)], axis=1).astype(BF16)

    hrows = red.shape[0] // 2
    swap = rcopy(red.at[pl.ds(pl.multiple_of(sib * hrows, 16), hrows)], redin, r_send, r_recv, c, sib)
    swap.start()

    def first_back(l):
        acc = None
        for da in range(3):
            term = dot(wb[da], mbx[own + l + 1 - da])
            acc = term if acc is None else acc + term
        ff = f1x[own + l, 64:128, 128:1152].astype(F32)
        return (shift_sum_back(acc, 64) * (1.0 - ff * ff)).astype(BF16)

    fbs[0] = first_back(0)
    swap.wait()
    half[...] = (red[pl.ds(pl.multiple_of(ax * hrows, 16), hrows)].astype(F32) + redin[...].astype(F32)).astype(BF16)

    def scatter(j):
        peer = lax.rem(c + j, n)
        return rcopy(half.at[pl.ds(pl.multiple_of(peer * chunk, 16), chunk)], hin.at[j],
                     s_send.at[j], s_recv.at[j], peer, ax)

    def start_scatter(j, carry):
        scatter(j).start()
        return carry

    lax.fori_loop(1, n, start_scatter, 0)

    fbs[1] = first_back(1)
    gf = None
    for l in range(2):
        xs = jnp.concatenate(
            [fs[own + l + da - 1, :, (2 + db) * 128 : (2 + db) * 128 + 1024]
             for da in range(3) for db in range(3)], axis=0)
        term = dot_nt(xs, fbs[l])
        gf = term if gf is None else gf + term
    gfp[0:128, 0:64] = gf[0:128]
    gfp[0:16, 64:128] = gf[128:144]

    def fscatter(j):
        peer = lax.rem(me + j, ndev)
        return pltpu.make_async_remote_copy(
            src_ref=gfp.at[pl.ds(pl.multiple_of(peer * fchunk, 8), fchunk)], dst_ref=gfin.at[j],
            send_sem=x_send.at[j], recv_sem=x_recv.at[j], device_id=device(peer), device_id_type=MESH)

    def start_fscatter(j, carry):
        fscatter(j).start()
        return carry

    lax.fori_loop(1, ndev, start_fscatter, 0)

    def add_chunk(j, total):
        scatter(j).wait()
        return total + hin[j].astype(F32)

    mine = half[pl.ds(pl.multiple_of(c * chunk, 16), chunk)].astype(F32)
    total = lax.fori_loop(1, n, add_chunk, mine)
    here = pl.multiple_of(c * chunk, 16)
    gat[ax, pl.ds(here, chunk)] = total.astype(BF16)

    def gather(j):
        part = gat.at[ax, pl.ds(here, chunk)]
        return rcopy(part, part, g_send.at[j], g_recv.at[j], lax.rem(c + j, n), ax)

    def start_gather(j, carry):
        gather(j).start()
        return carry

    lax.fori_loop(1, n, start_gather, 0)

    def forward(j):
        origin = lax.rem(c + n - j, n)
        part = gat.at[ax, pl.ds(pl.multiple_of(origin * chunk, 16), chunk)]
        return rcopy(part, part, h_send.at[j], h_recv.at[j], c, sib)

    forward(0).start()

    def fadd(j, total):
        fscatter(j).wait()
        return total + gfin[j]

    fmine = gfp[pl.ds(pl.multiple_of(me * fchunk, 8), fchunk)]
    fhere = pl.multiple_of(me * fchunk, 8)
    gfr[pl.ds(fhere, fchunk)] = lax.fori_loop(1, ndev, fadd, fmine)

    def fgather(j):
        peer = lax.rem(me + j, ndev)
        part = gfr.at[pl.ds(fhere, fchunk)]
        return pltpu.make_async_remote_copy(
            src_ref=part, dst_ref=part, send_sem=q_send.at[j], recv_sem=q_recv.at[j],
            device_id=device(peer), device_id_type=MESH)

    def start_fgather(j, carry):
        fgather(j).start()
        return carry

    lax.fori_loop(1, ndev, start_fgather, 0)

    def relay(j, carry):
        gather(j).wait()
        forward(j).start()
        return carry

    lax.fori_loop(1, n, relay, 0)

    def end_forward(j, carry):
        forward(j).wait()
        return carry

    lax.fori_loop(0, n, end_forward, 0)

    gat_out[...] = gat[...]

    def end_fgather(j, carry):
        fgather(j).wait()
        return carry

    lax.fori_loop(1, ndev, end_fgather, 0)
    gf_out[...] = gfr[...]


def unpack(pred_in, gf_in, gat_in, pred_out, gfirst_out, gmid_out, glast_out, gfirst_v, gmid_v, glast_v, sems):
    hrows = gat_in.shape[1]
    copies = [
        pltpu.make_async_copy(src, dst, sems.at[i])
        for i, (src, dst) in enumerate(
            ((pred_in, pred_out), (gfirst_v, gfirst_out), (gmid_v, gmid_out), (glast_v, glast_out)))
    ]
    copies[0].start()
    for dd in range(9):
        for ch in range(3):
            row = dd % 8 * 16 + ch * 3
            gfirst_v[ch, 3 * dd : 3 * dd + 3, :] = gf_in[row : row + 3, dd // 8 * 64 : dd // 8 * 64 + 64]
    copies[1].start()

    def rows_of(start, count, lanes):
        hr = hrows
        if start + count <= hr:
            return gat_in[0, start : start + count, lanes : lanes + 64]
        if start >= hr:
            return gat_in[1, start - hr : start - hr + count, lanes : lanes + 64]
        return jnp.concatenate(
            [gat_in[0, start:hr, lanes : lanes + 64], gat_in[1, 0 : start + count - hr, lanes : lanes + 64]], axis=0)

    for dd in range(9):
        if dd < 8:
            lblock = rows_of(864 + dd // 2 * 16, 16, dd % 2 * 64).astype(F32)
        else:
            lblock = rows_of(928, 16, 0).astype(F32)
        for dr in range(3):
            k = dd * 3 + dr
            glast_v[k] = lblock[dr * 4 : dr * 4 + 4]
            if dd < 8:
                gmid_v[k] = rows_of(dd // 2 * 192 + dr * 64, 64, dd % 2 * 64).astype(F32)
            elif dr == 0:
                gmid_v[k] = rows_of(768, 64, 0).astype(F32)
            elif dr == 1:
                gmid_v[k, 0:32] = rows_of(832, 32, 0).astype(F32)
                gmid_v[k, 32:64] = rows_of(768, 32, 64).astype(F32)
            else:
                gmid_v[k] = rows_of(800, 64, 64).astype(F32)
    copies[2].start()
    copies[3].start()
    for cp in copies:
        cp.wait()


def body(features, w_first, w_middle, w_last, diffusion, pressure, advection, forcing):
    n = lax.axis_size("circ")
    ndev = 2 * n
    rows, cols, depth = features.shape[1:]
    cells = rows * cols * depth * ndev
    chunk = max(16, 512 // n)
    rrows = chunk * n * 2
    fchunk = max(8, 128 // ndev)
    frows = fchunk * ndev

    V = pltpu.VMEM
    dma = pltpu.SemaphoreType.DMA
    scratch = [
        V((3, 192, 192), BF16), V((3, 192, 192), BF16), V((64, 144), BF16), V((3, 32, 192), BF16),
        V((64, 144), BF16), V((144, 128), F32), V((3, 32, 192), F32),
        V((2, 3, 2, 8, 128), F32), V((2, 3, 8, 128), F32), V((2, 3, 8, 128), F32),
        V((2, 12, 2, 8, 128), F32), V((2, 6, 16, 128), BF16), V((2, 6, 16, 128), BF16),
        V((2, 3, 8, 128), F32), V((2, 6, 16, 128), BF16),
        V((4, 8, 1792), F32), V((16, 1792), F32), V((6, 16, 1792), BF16),
        V((6, 192, 1280), BF16), V((4, 64, 1280), BF16), V((6, 192, 1024), BF16),
        V((4, 4, 8, 128), F32), V((2, 4, 2, 8, 128), F32), V((2, 4, 2, 8, 128), F32),
        V((4, 4, 16, 128), F32), V((4, 8, 1536), F32), V((6, 16, 1536), BF16),
        V((6, 192, 1024), BF16), V((2, 64, 1024), BF16),
        V((rrows, 128), BF16), V((rrows // 2, 128), BF16), V((rrows // 2, 128), BF16),
        V((n, chunk, 128), BF16), V((2, rrows // 2, 128), BF16),
        V((frows, 128), F32), V((ndev, fchunk, 128), F32), V((frows, 128), F32),
        dma((8,)), dma((8,)), dma((2,)), dma((2,)), dma, dma, dma((n,)), dma((n,)), dma((n,)), dma((n,)),
        dma((ndev,)), dma((ndev,)), dma((ndev,)), dma((ndev,)), dma((n,)), dma((n,)), dma((2,)), dma((2,)),
    ]
    vm = pl.BlockSpec(memory_space=pltpu.VMEM)
    pred, gf, gat = pl.pallas_call(
        functools.partial(kernel, n, cells, chunk, fchunk),
        out_shape=(
            jax.ShapeDtypeStruct((4, rows, cols, depth), BF16),
            jax.ShapeDtypeStruct((frows, 128), F32),
            jax.ShapeDtypeStruct((2, rrows // 2, 128), BF16),
        ),
        in_specs=[vm] * 8,
        out_specs=(vm,) * 3,
        scratch_shapes=scratch,
        compiler_params=pltpu.CompilerParams(
            collective_id=0, has_side_effects=True, vmem_limit_bytes=48 * 1024 * 1024),
    )(features, w_first.transpose(2, 0, 1), w_middle, w_last, diffusion, pressure, advection, forcing)
    hbm = pl.BlockSpec(memory_space=pl.ANY)
    predicted, gfirst, gmid, glast = pl.pallas_call(
        unpack,
        out_shape=(
            jax.ShapeDtypeStruct((4, rows, cols, depth), BF16),
            jax.ShapeDtypeStruct((3, 27, 64), F32),
            jax.ShapeDtypeStruct((27, 64, 64), F32),
            jax.ShapeDtypeStruct((27, 4, 64), F32),
        ),
        in_specs=[vm] * 3,
        out_specs=(hbm,) * 4,
        scratch_shapes=[V((3, 27, 64), F32), V((27, 64, 64), F32), V((27, 4, 64), F32), dma((4,))],
    )(pred, gf, gat)
    return predicted, gfirst.transpose(1, 2, 0), gmid, glast


def solution(mesh):
    field = P(None, ("group", "axial"), "circ", None)
    grad = P("group", None, None)
    return jax.shard_map(
        body,
        mesh=mesh,
        in_specs=(field, P(), P(), P(), field, field, field, field),
        out_specs=(field, grad, grad, grad),
        check_vma=False,
    )
```

```python
import functools

import jax
import jax.numpy as jnp
from jax import lax
from jax.experimental import pallas as pl
from jax.experimental.pallas import tpu as pltpu
from jax.sharding import PartitionSpec as P

MESH = pl.DeviceIdType.MESH
F32 = jnp.float32
BF16 = jnp.bfloat16
VMEM_LIMIT = 62 * 1024 * 1024


def dot(a, b):
    return jnp.dot(a, b, preferred_element_type=F32)


def dot_nt(a, b):
    return lax.dot_general(a, b, (((1,), (1,)), ((), ())), preferred_element_type=F32)


def from_behind(x):
    axis = x.ndim - 1
    lane = lax.broadcasted_iota(jnp.int32, x.shape, axis) % 128
    return jnp.where(lane == 0, 0.0, pltpu.roll(x, 1, axis))


def from_ahead(x):
    axis = x.ndim - 1
    lane = lax.broadcasted_iota(jnp.int32, x.shape, axis) % 128
    return jnp.where(lane == 127, 0.0, pltpu.roll(x, x.shape[axis] - 1, axis))


def shift_sum(z, rows):
    return from_behind(z[0:rows]) + z[rows : 2 * rows] + from_ahead(z[2 * rows : 3 * rows])


def shift_sum_back(z, rows):
    return from_ahead(z[0:rows]) + z[rows : 2 * rows] + from_behind(z[2 * rows : 3 * rows])


def ahead(x, d):
    if d == 0:
        return jnp.concatenate([x[1:], jnp.zeros_like(x[:1])], axis=0)
    if d == 1:
        return pltpu.roll(x, 15, 1)
    return from_ahead(x)


def behind(x, d):
    if d == 0:
        return jnp.concatenate([jnp.zeros_like(x[:1]), x[:-1]], axis=0)
    if d == 1:
        return pltpu.roll(x, 1, 1)
    return from_behind(x)


def low_half(x, y):
    sub = lax.broadcasted_iota(jnp.int32, x.shape, x.ndim - 2)
    return jnp.where(sub < 4, x, y)


def roll4(x):
    return pltpu.roll(x, 4, x.ndim - 2)


def pack_low(x0, x1):
    return low_half(x0, roll4(x1))


def pack_high(x0, x1):
    return low_half(roll4(x1), x0)


def halo_tiles(right, left):
    return low_half(right, left), roll4(low_half(left, right))


def kernel(n, cells, chunk, *refs):
    (*sources,
     pred_out, gat_out,
     feat, w1_in, wm_in, wl_in, diff, pres, adv, forc, i_sem,
     wf, wb, w1, w3, w3t, stage, w3s,
     fc, fr, fl, mc, mr, ml, fsend, msend, fbase, fstage, fs, f1x, mid, m1x, pc, ph, psend,
     ogs, obase, og, mbx, fbs,
     red, redin, half, hin, gat,
     a_send, a_recv, p_send, p_recv, r_send, r_recv, s_send, s_recv, g_send, g_recv,
     h_send, h_recv, m_send, m_recv) = refs
    c = lax.axis_index("circ")
    ax = lax.axis_index("axial")
    grp = lax.axis_index("group")
    sib = 1 - ax
    right = lax.rem(c + 1, n)
    left = lax.rem(c + n - 1, n)
    def rcopy(src, dst, ss, rs, circ, axial):
        return pltpu.make_async_remote_copy(
            src_ref=src, dst_ref=dst, send_sem=ss, recv_sem=rs,
            device_id=(grp, circ, axial), device_id_type=MESH)

    loads = [
        pltpu.make_async_copy(src, dst, i_sem.at[i])
        for i, (src, dst) in enumerate(zip(sources, (feat, w1_in, wm_in, wl_in, diff, pres, adv, forc)))
    ]
    for i in (0, 1, 4, 5, 6, 7, 2, 3):
        loads[i].start()

    barrier = pltpu.get_barrier_semaphore()

    def greet(j, carry):
        pl.semaphore_signal(barrier, inc=1, device_id=(grp, lax.rem(c + j, n), ax), device_id_type=MESH)
        return carry

    for cc in (left, right, c):
        pl.semaphore_signal(barrier, inc=1, device_id=(grp, cc, sib), device_id_type=MESH)
    lax.fori_loop(1, n, greet, 0)

    loads[0].wait()
    x = feat[...].astype(F32)
    fc[ax] = x
    fsend[0] = pack_low(x[:, 0], x[:, 1])
    fsend[1] = pack_high(x[:, 0], x[:, 1])
    lows, highs = [], []
    for g, ref in enumerate((diff, pres, adv, forc)):
        loads[4 + g].wait()
        x = ref[...]
        mc[ax, 3 * g : 3 * g + 3] = x
        for i in range(3):
            lows.append(pack_low(x[i, 0], x[i, 1]))
            highs.append(pack_high(x[i, 0], x[i, 1]))
    for i in range(6):
        msend[0, i] = jnp.concatenate(lows[2 * i : 2 * i + 2], axis=0).astype(BF16)
        msend[1, i] = jnp.concatenate(highs[2 * i : 2 * i + 2], axis=0).astype(BF16)

    stage[...] = jnp.zeros_like(stage)
    loads[1].wait()
    for ch in range(3):
        v = w1_in[ch].astype(F32)
        for dd in range(9):
            stage[dd * 16 + ch * 3 : dd * 16 + ch * 3 + 3, 0:64] = v[3 * dd : 3 * dd + 3]
    w1[...] = stage[...].T[0:64].astype(BF16)

    pl.semaphore_wait(barrier, n + 2)

    fcopies = []
    mcopies = []
    fcopies.append(rcopy(fc.at[ax], fc.at[ax], a_send.at[0], a_recv.at[0], c, sib))
    fcopies.append(rcopy(fsend.at[0], fr.at[ax], a_send.at[1], a_recv.at[1], left, ax))
    fcopies.append(rcopy(fsend.at[1], fl.at[ax], a_send.at[2], a_recv.at[2], right, ax))
    fcopies.append(rcopy(fsend.at[0], fr.at[ax], a_send.at[3], a_recv.at[3], left, sib))
    fcopies.append(rcopy(fsend.at[1], fl.at[ax], a_send.at[4], a_recv.at[4], right, sib))
    mcopies.append(rcopy(mc.at[ax], mc.at[ax], a_send.at[5], a_recv.at[5], c, sib))
    mcopies.append(rcopy(msend.at[0], mr.at[ax], a_send.at[6], a_recv.at[6], left, ax))
    mcopies.append(rcopy(msend.at[1], ml.at[ax], a_send.at[7], a_recv.at[7], right, ax))
    relays = [
        rcopy(mr.at[ax], mr.at[ax], m_send.at[0], m_recv.at[0], c, sib),
        rcopy(ml.at[ax], ml.at[ax], m_send.at[1], m_recv.at[1], c, sib),
    ]
    for cp in fcopies + mcopies:
        cp.start()

    loads[2].wait()
    loads[3].wait()
    for da in range(3):
        for dr in range(3):
            wf[da, dr * 64 : dr * 64 + 64] = jnp.concatenate(
                [wm_in[9 * da + 3 * db + dr] for db in range(3)], axis=1)
    w3s[...] = jnp.zeros_like(w3s)
    for da in range(3):
        for dr in range(3):
            w3s[da, dr * 8 : dr * 8 + 4] = jnp.concatenate(
                [wl_in[9 * da + 3 * db + dr].astype(F32) for db in range(3)], axis=1)
    w3[...] = w3s[...].astype(BF16)

    for ref in (fs, f1x, m1x, og, mbx):
        ref[0] = jnp.zeros_like(ref[0])
        ref[5] = jnp.zeros_like(ref[5])
    fstage[...] = jnp.zeros_like(fstage)
    if red.shape[0] > 1024:
        red[1024:] = jnp.zeros_like(red[1024:])
    fbase[...] = jnp.zeros_like(fbase)
    obase[...] = jnp.zeros_like(obase)

    for cp in fcopies:
        cp.wait()

    for a in range(4):
        slab, l = a // 2, a % 2
        for ch in range(3):
            for j in range(14):
                b = j - 3
                if b < 0:
                    row = (8 + b) - 4 + (4 if l == 0 else 0)
                    v = fl[slab, ch, row : row + 1, :]
                elif b > 7:
                    row = (b - 8) + 4 * l
                    v = fr[slab, ch, row : row + 1, :]
                else:
                    v = fc[slab, ch, l, b : b + 1, :]
                fbase[a, ch : ch + 1, j * 128 : (j + 1) * 128] = v
        base = fbase[a]
        low, high = from_behind(base), from_ahead(base)
        for ch in range(3):
            fstage[3 * ch : 3 * ch + 1, :] = low[ch : ch + 1]
            fstage[3 * ch + 1 : 3 * ch + 2, :] = base[ch : ch + 1]
            fstage[3 * ch + 2 : 3 * ch + 3, :] = high[ch : ch + 1]
        fs[a + 1] = fstage[...].astype(BF16)

    for a in range(4):
        xs = jnp.concatenate(
            [fs[a + da, :, db * 128 : db * 128 + 1536] for da in range(3) for db in range(3)], axis=0)
        first = jnp.tanh(dot(w1[...], xs)).astype(BF16)
        for db in range(3):
            f1x[a + 1, db * 64 : db * 64 + 64, :] = first[:, db * 128 : db * 128 + 1280]

    for cp in mcopies:
        cp.wait()
    for cp in relays:
        cp.start()

    for a in range(4):
        for t in range(5):
            acc = None
            for da in range(3):
                if 0 <= a + da - 1 < 4:
                    term = dot(wf[da], f1x[a + da, :, t * 256 : t * 256 + 256])
                    acc = term if acc is None else acc + term
            mid[a, :, t * 256 : t * 256 + 256] = jnp.tanh(shift_sum(acc, 64)).astype(BF16)
        for db in range(3):
            m1x[a + 1, db * 64 : db * 64 + 64, :] = mid[a, :, db * 128 : db * 128 + 1024]

    for a in range(4):
        acc = None
        for da in range(3):
            if 0 <= a + da - 1 < 4:
                term = dot(w3[da], m1x[a + da])
                acc = term if acc is None else acc + term
        y = shift_sum(acc, 8).astype(BF16).astype(F32)
        for ch in range(4):
            for b in range(8):
                pc[ch, a, b : b + 1, :] = y[ch : ch + 1, b * 128 : b * 128 + 128]
    q = pc[...]
    for s in range(2):
        psend[0, :, s] = pack_low(q[:, 2 * s], q[:, 2 * s + 1])
        psend[1, :, s] = pack_high(q[:, 2 * s], q[:, 2 * s + 1])
    pcopies = [
        rcopy(psend.at[0], ph.at[0], p_send.at[0], p_recv.at[0], left, ax),
        rcopy(psend.at[1], ph.at[1], p_send.at[1], p_recv.at[1], right, ax),
    ]
    for cp in pcopies:
        cp.start()
    pred_out[...] = pc[:, pl.ds(2 * ax, 2)].astype(BF16)
    for dd in range(9):
        for dr in range(3):
            stage[dd * 16 + dr * 4 : dd * 16 + dr * 4 + 4, 0:64] = wl_in[dd * 3 + dr].astype(F32)
        stage[dd * 16 + 12 : dd * 16 + 16, 0:64] = jnp.zeros((4, 64), F32)
    w3t[...] = stage[...].T[0:64].astype(BF16)
    for da in range(3):
        for dr in range(3):
            tall = jnp.concatenate([wm_in[9 * da + 3 * db + dr] for db in range(3)], axis=0)
            wb[da, dr * 64 : dr * 64 + 64] = tall.T
    for cp in relays:
        cp.wait()
    for cp in pcopies:
        cp.wait()

    def metric(index):
        layers = []
        for slab in range(2):
            h = halo_tiles(*(ref[slab, index // 2].astype(F32)[index % 2 * 8 : index % 2 * 8 + 8] for ref in (mr, ml)))
            for l in range(2):
                layers.append(jnp.concatenate([mc[slab, index, l], h[l]], axis=0))
        return jnp.stack(layers)

    field = []
    for ch in range(4):
        layers = []
        for s in range(2):
            h = halo_tiles(ph[0, ch, s], ph[1, ch, s])
            for l in range(2):
                layers.append(jnp.concatenate([pc[ch, 2 * s + l], h[l]], axis=0))
        field.append(jnp.stack(layers))
    D = [metric(d) for d in range(3)]
    A = [metric(6 + d) for d in range(3)]
    resid = [metric(9 + m) for m in range(3)]
    pm = [metric(3 + m) for m in range(3)]
    diffs = {}
    for m in range(3):
        for d in range(3):
            pa, pb = ahead(field[m], d), behind(field[m], d)
            diffs[m, d] = (pa - pb) * 0.5
            resid[m] = resid[m] + D[d] * (pa - 2.0 * field[m] + pb) - A[d] * field[d] * diffs[m, d]
        resid[m] = resid[m] - pm[m] * (ahead(field[3], m) - behind(field[3], m)) * 0.5
    t = [r / (3.0 * cells) for r in resid]
    out_p = None
    for m in range(3):
        total = None
        for d in range(3):
            dt = D[d] * t[m]
            y = A[d] * field[d] * t[m] * 0.5
            term = ahead(dt + y, d) + behind(dt - y, d) - 2.0 * dt
            total = term if total is None else total + term
        total = total - A[m] * (t[0] * diffs[0, m] + t[1] * diffs[1, m] + t[2] * diffs[2, m])
        ogs[m] = total
        y = pm[m] * t[m] * 0.5
        term = ahead(y, m) - behind(y, m)
        out_p = term if out_p is None else out_p + term
    ogs[3] = out_p

    fstage[0:16, :] = jnp.zeros((16, 1792), F32)
    for a in range(4):
        for ch in range(4):
            for j in range(12):
                b = (j - 2) % 16
                obase[a, ch : ch + 1, j * 128 : (j + 1) * 128] = ogs[ch, a, b : b + 1, :]
        base = obase[a]
        fstage[0:4, 0:1536] = from_ahead(base)[0:4]
        fstage[4:8, 0:1536] = base[0:4]
        fstage[8:12, 0:1536] = from_behind(base)[0:4]
        og[a + 1] = fstage[:, 0:1536].astype(BF16)

    for a in range(4):
        xs = jnp.concatenate(
            [og[a + 2 - da, :, (2 - db) * 128 : (2 - db) * 128 + 1280] for da in range(3) for db in range(3)],
            axis=0)
        mf = mid[a].astype(F32)
        back = (dot(w3t[...], xs) * (1.0 - mf * mf)).astype(BF16)
        for db in range(3):
            mbx[a + 1, db * 64 : db * 64 + 64, :] = back[:, (2 - db) * 128 : (2 - db) * 128 + 1024]

    own = 2 * ax + 1
    gm = [None] * 3
    gl = [None] * 3
    for l in range(2):
        m = mbx[own + l, 64:128, :].astype(F32)
        mbs = jnp.concatenate([from_ahead(m), m, from_behind(m)], axis=0).astype(BF16)
        ogo = og[own + l, :, 256:1280]
        for da in range(3):
            term = dot_nt(mbs, f1x[own + l + da - 1, :, 128:1152])
            gm[da] = term if gm[da] is None else gm[da] + term
            term = dot_nt(ogo, m1x[own + l + da - 1])
            gl[da] = term if gl[da] is None else gl[da] + term

    def block(parts, dd):
        return parts[dd // 3][:, dd % 3 * 64 : dd % 3 * 64 + 64]

    for p in range(4):
        red[p * 192 : p * 192 + 192] = jnp.concatenate(
            [block(gm, 2 * p), block(gm, 2 * p + 1)], axis=1).astype(BF16)
        red[864 + p * 16 : 880 + p * 16] = jnp.concatenate(
            [block(gl, 2 * p), block(gl, 2 * p + 1)], axis=1).astype(BF16)
    lastm, lastl = block(gm, 8), block(gl, 8)
    red[768:864] = jnp.concatenate([lastm[0:96], lastm[96:192]], axis=1).astype(BF16)
    red[928:944] = jnp.concatenate([lastl, jnp.zeros_like(lastl)], axis=1).astype(BF16)

    hrows = red.shape[0] // 2
    early = (944 - hrows) // chunk
    erows = early * chunk

    def swap(k):
        start, count = ((0, erows), (erows, hrows - erows))[k]
        return rcopy(red.at[pl.ds(pl.multiple_of(sib * hrows + start, 16), count)], redin.at[start : start + count],
                     r_send.at[k], r_recv.at[k], c, sib)

    def merge(k):
        start, count = ((0, erows), (erows, hrows - erows))[k]
        swap(k).wait()
        mine = red[pl.ds(pl.multiple_of(ax * hrows + start, 16), count)].astype(F32)
        half[start : start + count] = (mine + redin[start : start + count].astype(F32)).astype(BF16)

    def scatter(j):
        peer = lax.rem(c + j, n)
        return rcopy(half.at[pl.ds(pl.multiple_of(peer * chunk, 16), chunk)], hin.at[j],
                     s_send.at[j], s_recv.at[j], peer, ax)

    def start_scatter(first):
        def step(j, carry):
            @pl.when((lax.rem(c + j, n) < early) == first)
            def _():
                scatter(j).start()
            return carry

        lax.fori_loop(1, n, step, 0)

    swap(0).start()

    def first_back(l):
        acc = None
        for da in range(3):
            term = dot(wb[da], mbx[own + l + 1 - da])
            acc = term if acc is None else acc + term
        ff = f1x[own + l, 64:128, 128:1152].astype(F32)
        return (shift_sum_back(acc, 64) * (1.0 - ff * ff)).astype(BF16)

    fbs[0] = first_back(0)
    merge(0)
    start_scatter(True)
    fbs[1] = first_back(1)
    gf = None
    for l in range(2):
        xs = jnp.concatenate(
            [fs[own + l + da - 1, :, (2 + db) * 128 : (2 + db) * 128 + 1024]
             for da in range(3) for db in range(3)], axis=0)
        term = dot_nt(xs, fbs[l])
        gf = term if gf is None else gf + term
    tail = jnp.concatenate([gf[80:144], jnp.zeros((16, 64), F32)], axis=0)
    red[944:1024] = jnp.concatenate([gf[0:80], tail], axis=1).astype(BF16)
    swap(1).start()
    merge(1)
    start_scatter(False)

    def add_chunk(j, total):
        scatter(j).wait()
        return total + hin[j].astype(F32)

    mine = half[pl.ds(pl.multiple_of(c * chunk, 16), chunk)].astype(F32)
    total = lax.fori_loop(1, n, add_chunk, mine)
    here = pl.multiple_of(c * chunk, 16)
    gat[ax, pl.ds(here, chunk)] = total.astype(BF16)

    def gather(j):
        part = gat.at[ax, pl.ds(here, chunk)]
        return rcopy(part, part, g_send.at[j], g_recv.at[j], lax.rem(c + j, n), ax)

    def start_gather(j, carry):
        gather(j).start()
        return carry

    lax.fori_loop(1, n, start_gather, 0)

    def forward(j):
        origin = lax.rem(c + n - j, n)
        part = gat.at[ax, pl.ds(pl.multiple_of(origin * chunk, 16), chunk)]
        return rcopy(part, part, h_send.at[j], h_recv.at[j], c, sib)

    forward(0).start()

    def relay(j, carry):
        gather(j).wait()
        forward(j).start()
        return carry

    lax.fori_loop(1, n, relay, 0)

    def end_forward(j, carry):
        forward(j).wait()
        return carry

    lax.fori_loop(0, n, end_forward, 0)

    gat_out[...] = gat[...]


def unpack(pred_in, gat_hbm, pred_out, gfirst_out, gmid_out, glast_out, gat_in, gfirst_v, gmid_v, glast_v, sems):
    load = pltpu.make_async_copy(gat_hbm, gat_in, sems.at[4])
    load.start()
    hrows = gat_in.shape[1]
    copies = [
        pltpu.make_async_copy(src, dst, sems.at[i])
        for i, (src, dst) in enumerate(
            ((pred_in, pred_out), (gfirst_v, gfirst_out), (gmid_v, gmid_out), (glast_v, glast_out)))
    ]
    copies[0].start()
    load.wait()
    def rows_of(start, count, lanes):
        hr = hrows
        if start + count <= hr:
            return gat_in[0, start : start + count, lanes : lanes + 64]
        if start >= hr:
            return gat_in[1, start - hr : start - hr + count, lanes : lanes + 64]
        return jnp.concatenate(
            [gat_in[0, start:hr, lanes : lanes + 64], gat_in[1, 0 : start + count - hr, lanes : lanes + 64]], axis=0)

    for dd in range(9):
        if dd < 8:
            lblock = rows_of(864 + dd // 2 * 16, 16, dd % 2 * 64).astype(F32)
        else:
            lblock = rows_of(928, 16, 0).astype(F32)
        for dr in range(3):
            k = dd * 3 + dr
            glast_v[k] = lblock[dr * 4 : dr * 4 + 4]
            if dd < 8:
                gmid_v[k] = rows_of(dd // 2 * 192 + dr * 64, 64, dd % 2 * 64).astype(F32)
            elif dr == 0:
                gmid_v[k] = rows_of(768, 64, 0).astype(F32)
            elif dr == 1:
                gmid_v[k, 0:32] = rows_of(832, 32, 0).astype(F32)
                gmid_v[k, 32:64] = rows_of(768, 32, 64).astype(F32)
            else:
                gmid_v[k] = rows_of(800, 64, 64).astype(F32)
    copies[2].start()
    g0 = rows_of(944, 80, 0).astype(F32)
    g1 = rows_of(944, 64, 64).astype(F32)
    for dd in range(9):
        for ch in range(3):
            row = dd % 5 * 16 + ch * 3
            gfirst_v[ch, 3 * dd : 3 * dd + 3, :] = (g0 if dd < 5 else g1)[row : row + 3]
    copies[1].start()
    copies[3].start()
    for cp in copies:
        cp.wait()


def body(features, w_first, w_middle, w_last, diffusion, pressure, advection, forcing):
    n = lax.axis_size("circ")
    rows, cols, depth = features.shape[1:]
    cells = rows * cols * depth * n * 2
    chunk = max(16, 512 // n)
    rrows = chunk * n * 2

    V = pltpu.VMEM
    dma = pltpu.SemaphoreType.DMA
    held = (features, w_first.transpose(2, 0, 1), w_middle, w_last, diffusion, pressure, advection, forcing)
    scratch = [V(x.shape, x.dtype) for x in held] + [
        dma((8,)),
        V((3, 192, 192), BF16), V((3, 192, 192), BF16), V((64, 144), BF16), V((3, 32, 192), BF16),
        V((64, 144), BF16), V((144, 128), F32), V((3, 32, 192), F32),
        V((2, 3, 2, 8, 128), F32), V((2, 3, 8, 128), F32), V((2, 3, 8, 128), F32),
        V((2, 12, 2, 8, 128), F32), V((2, 6, 16, 128), BF16), V((2, 6, 16, 128), BF16),
        V((2, 3, 8, 128), F32), V((2, 6, 16, 128), BF16),
        V((4, 8, 1792), F32), V((16, 1792), F32), V((6, 16, 1792), BF16),
        V((6, 192, 1280), BF16), V((4, 64, 1280), BF16), V((6, 192, 1024), BF16),
        V((4, 4, 8, 128), F32), V((2, 4, 2, 8, 128), F32), V((2, 4, 2, 8, 128), F32),
        V((4, 4, 16, 128), F32), V((4, 8, 1536), F32), V((6, 16, 1536), BF16),
        V((6, 192, 1024), BF16), V((2, 64, 1024), BF16),
        V((rrows, 128), BF16), V((rrows // 2, 128), BF16), V((rrows // 2, 128), BF16),
        V((n, chunk, 128), BF16), V((2, rrows // 2, 128), BF16),
        dma((8,)), dma((8,)), dma((2,)), dma((2,)), dma((2,)), dma((2,)), dma((n,)), dma((n,)), dma((n,)), dma((n,)),
        dma((n,)), dma((n,)), dma((2,)), dma((2,)),
    ]
    vm = pl.BlockSpec(memory_space=pltpu.VMEM)
    pred, gat = pl.pallas_call(
        functools.partial(kernel, n, cells, chunk),
        out_shape=(
            jax.ShapeDtypeStruct((4, rows, cols, depth), BF16),
            jax.ShapeDtypeStruct((2, rrows // 2, 128), BF16),
        ),
        in_specs=[pl.BlockSpec(memory_space=pltpu.HBM)] * 8,
        out_specs=(vm,) * 2,
        scratch_shapes=scratch,
        compiler_params=pltpu.CompilerParams(
            collective_id=0, has_side_effects=True, vmem_limit_bytes=VMEM_LIMIT),
    )(*held)
    hbm = pl.BlockSpec(memory_space=pl.ANY)
    predicted, gfirst, gmid, glast = pl.pallas_call(
        unpack,
        out_shape=(
            jax.ShapeDtypeStruct((4, rows, cols, depth), BF16),
            jax.ShapeDtypeStruct((3, 27, 64), F32),
            jax.ShapeDtypeStruct((27, 64, 64), F32),
            jax.ShapeDtypeStruct((27, 4, 64), F32),
        ),
        in_specs=[pl.BlockSpec(memory_space=pltpu.HBM)] * 2,
        out_specs=(hbm,) * 4,
        scratch_shapes=[
            V(gat.shape, BF16), V((3, 27, 64), F32), V((27, 64, 64), F32), V((27, 4, 64), F32), dma((5,))],
        compiler_params=pltpu.CompilerParams(vmem_limit_bytes=VMEM_LIMIT),
    )(pred, gat)
    return predicted, gfirst.transpose(1, 2, 0), gmid, glast


def solution(mesh):
    field = P(None, ("group", "axial"), "circ", None)
    grad = P("group", None, None)
    return jax.shard_map(
        body,
        mesh=mesh,
        in_specs=(field, P(), P(), P(), field, field, field, field),
        out_specs=(field, grad, grad, grad),
        check_vma=False,
    )
```
